32 devices in a mesh: win: 2 (over y), tile: 4 (over z), chan: 2 (over x), col: 2 (over core).
Axes of the slice: x: 2, y: 2, z: 4, core: 2. Of those that a mesh axis runs over, the one named last changes fastest.
Arguments:
- spectral_cube: float32 [2, 128, 128, 1024], P('chan', 'tile', 'win', 'col'), parts along dimension 2, may hold values from -32 to 32, as said below
- line_free: int32 [8, 256], P('win'), parts along dimension 0, may hold values from 0 to 1, as said below
- bad_flags: int32 [512], P('win'), parts along dimension 0, may hold values from 0 to 1, as said below
- kernel_widths: int32 [3], replicated, may hold values from 1 to 4
Outputs:
- significance: float32 [3, 256, 128, 1024], P(None, 'chan', ('win', 'tile'), 'col'), parts along dimension 2
The draws below stay inside these ranges and needn't reach their ends.
There are 2 independent parts, one for each index of `win`. The reference program is written for one: setup_inputs(seed, part) draws one part's arguments, and reference() takes and returns one part's arrays. A program takes and returns all parts, laid end to end along the dimension named above; an argument that names none is the same for every part. Nothing has to cross between parts.
Inputs may be any that keep to these rules, and one draw needn't show every extreme that they name: `spectral_cube`: brightness is a per-pixel cubic continuum plus channel noise. `line_free`: in each block of 16 rows the zeros form one run of 64 channels; in even-numbered blocks the run lies in the lower half of the channels, in odd-numbered blocks in the upper half. `bad_flags`: exactly 16 channels are flagged.
All inputs are finite; a program needn't handle non-finite values.
Results may differ from the reference program's by a relative error of at most 0.0003.
Values sent between devices are 32-bit elements; how exact they have to be, the bound alone decides.
A program may use at most 64 MiB of HBM per device.

```python
import math
import jax
import jax.numpy as jnp
from jax import lax

C = 256
HALF = 8
REG = 16
KERNELS = 3
H = 64
W = 1024
CHG = 128
NREG = 4


def draw_spectral_cube(key, part):
    key_coeff, key_noise, key_scale = jax.random.split(key, 3)
    coords = 2.0 * jnp.arange(C).astype(jnp.float32) / (C - 1) - 1.0
    basis_all = jnp.stack([jnp.ones_like(coords), coords, 1.5 * coords * coords - 0.5, 2.5 * coords * coords * coords - 1.5 * coords])
    amplitudes = jnp.array([1.0, 0.5, 0.3, 0.2], jnp.float32)
    coeffs = jax.random.truncated_normal(key_coeff, -3.0, 3.0, (4, H, W), jnp.float32) * amplitudes[:, None, None]
    levels = jnp.exp(jax.random.uniform(key_scale, (C,), jnp.float32, math.log(0.5), math.log(2.0)))
    channel_noise = jax.random.truncated_normal(key_noise, -4.0, 4.0, (C, H, W), jnp.float32) * levels[:, None, None]
    continuum = jnp.einsum('ic,ihw->chw', basis_all, coeffs)
    return (continuum + channel_noise).reshape(C // CHG, CHG, H, W)


def draw_line_free(key, part):
    key_low, key_high = jax.random.split(jax.random.fold_in(key, 11), 2)
    starts_low = jax.random.randint(key_low, (NREG,), 0, C // 4 + 1)
    starts_high = jax.random.randint(key_high, (NREG,), C // 2, 3 * C // 4 + 1)
    parity = jnp.arange(NREG) % 2
    starts = jnp.where(parity == 0, starts_low, starts_high)
    channels = jnp.arange(C)[None, :]
    inside = (channels >= starts[:, None]) & (channels < starts[:, None] + C // 4)
    return jnp.where(inside, 0, 1).astype(jnp.int32)


def draw_bad_flags(key, part):
    order = jax.random.permutation(jax.random.fold_in(key, 23), C)
    return (order < C // 16).astype(jnp.int32)


def setup_inputs(seed: int = 0, part: int = 0) -> dict:
    seeds = jax.random.split(jax.random.key(seed), 5)
    part_splits = jax.random.split(jax.random.fold_in(seeds[4], part), 5)
    spectral_cube = draw_spectral_cube(jax.random.fold_in(jax.random.fold_in(seeds[4], part), 71), part)
    line_free = draw_line_free(jax.random.fold_in(jax.random.fold_in(seeds[4], part), 71), part)
    bad_flags = draw_bad_flags(jax.random.fold_in(jax.random.fold_in(seeds[4], part), 71), part)
    kernel_widths = jax.random.randint(seeds[3], (KERNELS,), 1, 5).astype(jnp.int32)
    return dict(spectral_cube=spectral_cube, line_free=line_free, bad_flags=bad_flags, kernel_widths=kernel_widths)


highest = lax.Precision.HIGHEST

def legendre(coords):
    return jnp.stack([jnp.ones_like(coords), coords, 1.5 * coords * coords - 0.5, 2.5 * coords * coords * coords - 1.5 * coords])

def channel_coords(indices, channel_total):
    return 2.0 * indices.astype(jnp.float32) / (channel_total - 1) - 1.0

def invert_small(matrices):
    dimension = matrices.shape[-1]
    identity = jnp.broadcast_to(jnp.eye(dimension, dtype=matrices.dtype), matrices.shape)
    augmented = jnp.concatenate([matrices, identity], axis=2)
    for pivot_at in range(dimension):
        pivot_row = augmented[:, pivot_at, :] / augmented[:, pivot_at, pivot_at:pivot_at + 1]
        updated = augmented - augmented[:, :, pivot_at:pivot_at + 1] * pivot_row[:, None, :]
        chosen = (jnp.arange(dimension) == pivot_at)[None, :, None]
        augmented = jnp.where(chosen, pivot_row[:, None, :], updated)
    return augmented[:, :, dimension:]

def gaussian_taps(kernel_widths):
    offsets = jnp.arange(-HALF, HALF + 1).astype(jnp.float32)
    sigmas = kernel_widths.astype(jnp.float32)
    unscaled = jnp.exp(-offsets[None, :] * offsets[None, :] / (2.0 * sigmas[:, None] * sigmas[:, None]))
    return unscaled / lax.optimization_barrier(jnp.sum(unscaled, axis=1, keepdims=True))

def median_three(edge_levels):
    below_level = edge_levels[:, :-2]
    middle = edge_levels[:, 1:-1]
    above_level = edge_levels[:, 2:]
    highest_one = jnp.maximum(jnp.maximum(below_level, middle), above_level)
    lowest_one = jnp.minimum(jnp.minimum(below_level, middle), above_level)
    return below_level + middle + above_level - highest_one - lowest_one

def reference(spectral_cube, line_free, bad_flags, kernel_widths):
    spectra = spectral_cube.reshape(C, H, W)
    basis_all = legendre(channel_coords(jnp.arange(C), C))
    good_mask = (1 - bad_flags).astype(jnp.float32)
    free_mask = line_free.astype(jnp.float32)
    weights = free_mask * good_mask[None, :]
    normal_matrix = jnp.einsum('rc,ic,jc->rij', weights, basis_all, basis_all, precision=highest)
    inverse = invert_small(normal_matrix)
    weight_rows = jnp.repeat(weights, REG, axis=0)
    moments = jnp.einsum('ic,chw->ihw', basis_all, spectra * weight_rows.T[:, :, None], precision=highest)
    inverse_rows = jnp.repeat(inverse, REG, axis=0)
    coeffs = jnp.einsum('hij,jhw->ihw', inverse_rows, moments, precision=highest)
    residual = spectra - jnp.einsum('ic,ihw->chw', basis_all, coeffs, precision=highest)
    kernel_taps = gaussian_taps(kernel_widths)
    padded = jnp.pad(residual, ((0, 0), (HALF, HALF), (HALF, HALF)))
    free_rows = jnp.repeat(free_mask, REG, axis=0).T

    def smooth_one(tap_row):
        across = tap_row[0] * padded[:, :, 0:W]
        for offset in range(1, 2 * HALF + 1):
            across = across + tap_row[offset] * padded[:, :, offset:offset + W]
        both_axes = tap_row[0] * across[:, 0:H, :]
        for offset in range(1, 2 * HALF + 1):
            both_axes = both_axes + tap_row[offset] * across[:, offset:offset + H, :]
        line_power = lax.optimization_barrier(jnp.sum(free_rows[:, :, None] * both_axes * both_axes, axis=(1, 2)))
        return (both_axes, line_power)
    smoothed, line_power = lax.map(smooth_one, kernel_taps)
    counts = REG * W * lax.optimization_barrier(jnp.sum(free_mask, axis=0))
    noise_level = jnp.sqrt(line_power / counts[None, :] + 1e-06)
    edge_levels = jnp.pad(noise_level, ((0, 0), (1, 1)))
    noise_floor = median_three(edge_levels)
    return smoothed * good_mask[None, :, None, None] / noise_floor[:, :, None, None]
```

```python
import functools

import jax
import jax.numpy as jnp
from jax import lax
from jax.experimental import pallas as pl
from jax.experimental.pallas import tpu as pltpu
from jax.sharding import PartitionSpec as P

HALF = 8
REG = 16


highest = lax.Precision.HIGHEST


def neighbour_slabs(shard, axis, dim, width):
    size, length = (lax.axis_size(axis), shard.shape[dim])
    up = [(i, (i + 1) % size) for i in range(size - 1)]
    down = [(j, i) for i, j in up]
    last = lax.slice_in_dim(shard, length - width, length, axis=dim)
    leading = lax.slice_in_dim(shard, 0, width, axis=dim)
    return lax.ppermute(last, axis, up), lax.ppermute(leading, axis, down)


def sum_over(values, axis):
    if lax.axis_size(axis) == 2:
        return values + lax.ppermute(values, axis, [(0, 1), (1, 0)])
    return lax.psum(values, axis)


def split(values):
    high = values.astype(jnp.bfloat16)
    return high, (values - high.astype(jnp.float32)).astype(jnp.bfloat16)


def dot3(a, b):
    dot = functools.partial(jnp.dot, preferred_element_type=jnp.float32)
    return dot(a[0], b[0]) + (dot(a[0], b[1]) + dot(a[1], b[0]))


def smooth_kernel(
    sub, up_ref, mid_ref, down_ref, left_ref, right_ref, row_ref, col_ref, free_ref,
    out_ref, power_ref, row_high, row_low, col_high, col_low,
):
    kernels, channels, rows, cols = out_ref.shape
    slab = left_ref.shape[2]
    width = col_ref.shape[2]

    @pl.when(pl.program_id(0) == 0)
    def _():
        row_high[...], row_low[...] = split(row_ref[...])
        col_high[...], col_low[...] = split(col_ref[...])

    row_pair = (row_high[...], row_low[...])
    smooth_rows = []
    for first in range(0, channels, sub):
        def flat(ref):
            part = ref[:, first : first + sub, :]
            return part.reshape(part.shape[0] * sub, part.shape[2])

        middle = jnp.concatenate([flat(up_ref), flat(mid_ref), flat(down_ref)], axis=0)
        block = jnp.concatenate([flat(left_ref), middle, flat(right_ref)], axis=1)
        smooth_rows.append(split(dot3(row_pair, split(block))))
    size = sub * rows
    for kernel_at in range(kernels):
        part = slice(kernel_at * size, (kernel_at + 1) * size)
        high = jnp.concatenate([pair[0][part] for pair in smooth_rows], axis=0)
        low = jnp.concatenate([pair[1][part] for pair in smooth_rows], axis=0)
        col_pair = (col_high[kernel_at], col_low[kernel_at])
        total = jnp.zeros((channels, rows, 128), jnp.float32)
        for start in range(0, cols, width):
            window = slice(start, start + width + 2 * slab)
            smooth = dot3((high[:, window], low[:, window]), col_pair)
            smooth = smooth.reshape(channels, rows, width)
            out_ref[kernel_at, :, :, start : start + width] = smooth
            for lane in range(0, width, 128):
                piece = smooth[:, :, lane : lane + 128]
                total = total + piece * piece
        power_ref[kernel_at] = jnp.sum(total * free_ref[...], axis=1)


def smooth_call(up, middle, down, left, right, row_band, col_band, free_lanes):
    rows, channels, cols = middle.shape
    kernels = col_band.shape[0]
    slab = left.shape[2]
    padded_rows = left.shape[0]
    sub = 8
    step = 32 if channels % 32 == 0 else 8

    def by_channel(height, width):
        return pl.BlockSpec((height, step, width), lambda i: (0, i, 0))

    row_shape, col_shape = row_band.shape, col_band.shape
    return pl.pallas_call(
        functools.partial(smooth_kernel, sub),
        grid=(channels // step,),
        out_shape=(
            jax.ShapeDtypeStruct((kernels, channels, rows, cols), jnp.float32),
            jax.ShapeDtypeStruct((kernels, channels, 128), jnp.float32),
        ),
        in_specs=[
            by_channel(HALF, cols),
            by_channel(rows, cols),
            by_channel(HALF, cols),
            by_channel(padded_rows, slab),
            by_channel(padded_rows, slab),
            pl.BlockSpec(row_shape, lambda i: (0, 0)),
            pl.BlockSpec(col_shape, lambda i: (0, 0, 0)),
            pl.BlockSpec((step, rows, 128), lambda i: (i, 0, 0)),
        ],
        out_specs=(
            pl.BlockSpec((kernels, step, rows, cols), lambda i: (0, i, 0, 0)),
            pl.BlockSpec((kernels, step, 128), lambda i: (0, i, 0)),
        ),
        scratch_shapes=[
            pltpu.VMEM(row_shape, jnp.bfloat16),
            pltpu.VMEM(row_shape, jnp.bfloat16),
            pltpu.VMEM(col_shape, jnp.bfloat16),
            pltpu.VMEM(col_shape, jnp.bfloat16),
        ],
        compiler_params=pltpu.CompilerParams(vmem_limit_bytes=48 * 1024 * 1024),
        cost_estimate=pl.CostEstimate(
            flops=12 * kernels * channels * rows * cols * 512,
            bytes_accessed=4 * channels * cols * (padded_rows + kernels * rows),
            transcendentals=0,
        ),
    )(up, middle, down, left, right, row_band, col_band, free_lanes)


def legendre(coords):
    return jnp.stack(
        [
            jnp.ones_like(coords),
            coords,
            1.5 * coords * coords - 0.5,
            2.5 * coords * coords * coords - 1.5 * coords,
        ]
    )


def channel_coords(indices, channel_total):
    return 2.0 * indices.astype(jnp.float32) / (channel_total - 1) - 1.0


def invert_small(matrices):
    dimension = matrices.shape[-1]
    identity = jnp.broadcast_to(jnp.eye(dimension, dtype=matrices.dtype), matrices.shape)
    augmented = jnp.concatenate([matrices, identity], axis=2)
    for pivot_at in range(dimension):
        pivot_row = augmented[:, pivot_at, :] / augmented[:, pivot_at, pivot_at : pivot_at + 1]
        updated = augmented - augmented[:, :, pivot_at : pivot_at + 1] * pivot_row[:, None, :]
        chosen = (jnp.arange(dimension) == pivot_at)[None, :, None]
        augmented = jnp.where(chosen, pivot_row[:, None, :], updated)
    return augmented[:, :, dimension:]


def gaussian_taps(kernel_widths):
    offsets = jnp.arange(-HALF, HALF + 1).astype(jnp.float32)
    sigmas = kernel_widths.astype(jnp.float32)
    unscaled = jnp.exp(
        -offsets[None, :] * offsets[None, :] / (2.0 * sigmas[:, None] * sigmas[:, None])
    )
    return unscaled / jnp.sum(unscaled, axis=1, keepdims=True)


def median_three(edge_levels):
    below_level = edge_levels[:, :-2]
    middle = edge_levels[:, 1:-1]
    above_level = edge_levels[:, 2:]
    highest_one = jnp.maximum(jnp.maximum(below_level, middle), above_level)
    lowest_one = jnp.minimum(jnp.minimum(below_level, middle), above_level)
    return below_level + middle + above_level - highest_one - lowest_one


def band_matrices(taps, differences):
    band = jnp.zeros((taps.shape[0],) + differences.shape, jnp.float32)
    for offset in range(2 * HALF + 1):
        band = band + jnp.where(differences == offset, taps[:, offset][:, None, None], 0.0)
    return band


def body(spectral_cube, line_free, bad_flags, kernel_widths):
    tile_count = lax.axis_size("tile")
    tile_at = lax.axis_index("tile")
    chan_at = lax.axis_index("chan")
    sub_count = spectral_cube.shape[1]
    group_size = sub_count * tile_count
    full_rows = spectral_cube.shape[2]
    local_rows = full_rows // tile_count
    local_cols = spectral_cube.shape[3]
    channel_total = line_free.shape[1]
    good_mask = (1 - bad_flags).astype(jnp.float32)
    free_mask = line_free.astype(jnp.float32)
    weights = free_mask * good_mask[None, :]
    basis_all = legendre(channel_coords(jnp.arange(channel_total), channel_total))
    normal_matrix = jnp.einsum("rc,ic,jc->rij", weights, basis_all, basis_all, precision=highest)
    inverse_rows = jnp.repeat(invert_small(normal_matrix), REG, axis=0)
    group_first = chan_at * group_size
    row_first = tile_at * local_rows
    basis_group = lax.dynamic_slice_in_dim(basis_all, group_first, group_size, 1)
    weight_all_rows = jnp.repeat(weights, REG, axis=0)
    inverse_local = lax.dynamic_slice_in_dim(inverse_rows, row_first, local_rows, 0)
    received = lax.all_to_all(spectral_cube, "tile", split_axis=2, concat_axis=1, tiled=True)[0]
    weight_local = lax.dynamic_slice_in_dim(
        lax.dynamic_slice_in_dim(weight_all_rows, row_first, local_rows, 0),
        group_first,
        group_size,
        1,
    )
    block_moments = jnp.einsum(
        "ic,chw->ihw", basis_group, received * weight_local.T[:, :, None], precision=highest
    )
    row_share = sum_over(block_moments, "chan")
    coeffs = jnp.einsum("hij,jhw->ihw", inverse_local, row_share, precision=highest)
    continuum = jnp.einsum("ic,ihw->hcw", basis_group, coeffs, precision=highest)
    residual = jnp.transpose(received, (1, 0, 2)) - continuum
    slab = 128
    width = 256 if local_cols % 256 == 0 else 128
    sub = 8
    up, down = neighbour_slabs(residual, "tile", 0, HALF)
    edges = [
        jnp.concatenate([part[:, :, edge] for part in (up, residual, down)], axis=0)
        for edge in (slice(local_cols - slab, local_cols), slice(0, slab))
    ]
    col_size = lax.axis_size("col")
    onward = [(i, i + 1) for i in range(col_size - 1)]
    left = lax.ppermute(edges[0], "col", onward)
    right = lax.ppermute(edges[1], "col", [(j, i) for i, j in onward])
    kernel_taps = gaussian_taps(kernel_widths)
    kernels = kernel_taps.shape[0]
    padded_rows = local_rows + 2 * HALF
    column_diff = (
        jnp.arange(width + 2 * slab)[:, None] - jnp.arange(width)[None, :] - slab + HALF
    )
    row_diff = jnp.arange(padded_rows)[None, :] - jnp.arange(local_rows)[:, None]
    col_band = band_matrices(kernel_taps, column_diff)
    row_band = band_matrices(kernel_taps, row_diff)
    same = jnp.eye(sub, dtype=jnp.float32)
    row_band = (
        row_band[:, None, :, :, None] * same[None, :, None, None, :]
    ).reshape(kernels * sub * local_rows, padded_rows * sub)
    free_rows = jnp.repeat(free_mask, REG, axis=0)
    free_local = lax.dynamic_slice_in_dim(
        lax.dynamic_slice_in_dim(free_rows, row_first, local_rows, 0), group_first, group_size, 1
    ).T
    free_lanes = jnp.broadcast_to(free_local[:, :, None], free_local.shape + (128,))
    smoothed, power = smooth_call(
        up, residual, down, left, right, row_band, col_band, free_lanes
    )
    line_power = lax.psum(jnp.sum(power, axis=2), ("tile", "col"))
    counts_all = REG * local_cols * lax.axis_size("col") * jnp.sum(free_mask, axis=0)
    counts = lax.dynamic_slice_in_dim(counts_all, group_first, group_size, 0)
    noise_level = jnp.sqrt(line_power / counts[None, :] + 1e-06)
    below, above = neighbour_slabs(noise_level, "chan", 1, 1)
    edge_levels = jnp.concatenate([below, noise_level, above], axis=1)
    noise_floor = median_three(edge_levels)
    good_group = lax.dynamic_slice_in_dim(good_mask, group_first, group_size, 0)
    return smoothed * (good_group[None, :] / noise_floor)[:, :, None, None]


def solution(mesh):
    return jax.shard_map(
        body,
        mesh=mesh,
        in_specs=(P("chan", "tile", "win", "col"), P("win", None), P("win"), P()),
        out_specs=P(None, "chan", ("win", "tile"), "col"),
        check_vma=False,
    )
```

```python
import functools

import jax
import jax.numpy as jnp
from jax import lax
from jax.experimental import pallas as pl
from jax.experimental.pallas import tpu as pltpu
from jax.sharding import PartitionSpec as P

HALF = 8
REG = 16


highest = lax.Precision.HIGHEST


def neighbour_slabs(shard, axis, dim, width):
    size, length = (lax.axis_size(axis), shard.shape[dim])
    up = [(i, (i + 1) % size) for i in range(size - 1)]
    down = [(j, i) for i, j in up]
    last = lax.slice_in_dim(shard, length - width, length, axis=dim)
    leading = lax.slice_in_dim(shard, 0, width, axis=dim)
    return lax.ppermute(last, axis, up), lax.ppermute(leading, axis, down)


def sum_over(values, axis, most=2):
    size = lax.axis_size(axis)
    if size > most or size & (size - 1):
        return lax.psum(values, axis)
    stride = 1
    while stride < size:
        pairs = [(i, i ^ stride) for i in range(size)]
        values = values + lax.ppermute(values, axis, pairs)
        stride *= 2
    return values


def split(values):
    high = values.astype(jnp.bfloat16)
    return high, (values - high.astype(jnp.float32)).astype(jnp.bfloat16)


def dot3(a, b):
    dot = functools.partial(jnp.dot, preferred_element_type=jnp.float32)
    return dot(a[0], b[0]) + (dot(a[0], b[1]) + dot(a[1], b[0]))


def smooth_kernel(
    sub, up_ref, mid_ref, down_ref, left_ref, right_ref, row_ref, col_ref, free_ref, *rest
):
    out_ref, power_ref, row_high, row_low, col_high, col_low = rest[-6:]
    kernels, channels, rows, cols = out_ref.shape
    slab = left_ref.shape[2]
    width = col_ref.shape[2]

    row_high[...], row_low[...] = split(row_ref[...])
    col_high[...], col_low[...] = split(col_ref[...])
    row_pair = (row_high[...], row_low[...])
    smooth_rows = []
    for first in range(0, channels, sub):
        def flat(ref):
            part = ref[:, first : first + sub, :]
            return part.reshape(part.shape[0] * sub, part.shape[2])

        middle = jnp.concatenate([flat(up_ref), flat(mid_ref), flat(down_ref)], axis=0)
        block = jnp.concatenate([flat(left_ref), middle, flat(right_ref)], axis=1)
        smooth_rows.append(split(dot3(row_pair, split(block))))
    size = sub * rows
    for kernel_at in range(kernels):
        part = slice(kernel_at * size, (kernel_at + 1) * size)
        high = jnp.concatenate([pair[0][part] for pair in smooth_rows], axis=0)
        low = jnp.concatenate([pair[1][part] for pair in smooth_rows], axis=0)
        col_pair = (col_high[kernel_at], col_low[kernel_at])
        total = jnp.zeros((channels, rows, 128), jnp.float32)
        for start in range(0, cols, width):
            window = slice(start, start + width + 2 * slab)
            smooth = dot3((high[:, window], low[:, window]), col_pair)
            smooth = smooth.reshape(channels, rows, width)
            out_ref[kernel_at, :, :, start : start + width] = smooth
            for lane in range(0, width, 128):
                piece = smooth[:, :, lane : lane + 128]
                total = total + piece * piece
        power_ref[kernel_at] = jnp.sum(total * free_ref[...], axis=1)


def smooth_call(chunk, up, middle, down, left, right, row_band, col_band, free_lanes, so_far):
    rows, channels, cols = middle.shape
    kernels = col_band.shape[0]
    padded_rows, step, slab = left.shape
    sub = 8

    def whole(height, width):
        return pl.BlockSpec((height, step, width), lambda i: (0, 0, 0))

    row_shape, col_shape = row_band.shape, col_band.shape
    return pl.pallas_call(
        functools.partial(smooth_kernel, sub),
        grid=(1,),
        out_shape=(
            jax.ShapeDtypeStruct((kernels, channels, rows, cols), jnp.float32),
            jax.ShapeDtypeStruct((kernels, step, 128), jnp.float32),
        ),
        in_specs=[
            whole(HALF, cols),
            pl.BlockSpec((rows, step, cols), lambda i: (0, chunk, 0)),
            whole(HALF, cols),
            whole(padded_rows, slab),
            whole(padded_rows, slab),
            pl.BlockSpec(row_shape, lambda i: (0, 0)),
            pl.BlockSpec(col_shape, lambda i: (0, 0, 0)),
            pl.BlockSpec((step, rows, 128), lambda i: (chunk, 0, 0)),
        ]
        + [pl.BlockSpec(memory_space=pl.ANY)] * len(so_far),
        out_specs=(
            pl.BlockSpec((kernels, step, rows, cols), lambda i: (0, chunk, 0, 0)),
            pl.BlockSpec((kernels, step, 128), lambda i: (0, 0, 0)),
        ),
        input_output_aliases={8: 0} if so_far else {},
        scratch_shapes=[
            pltpu.VMEM(row_shape, jnp.bfloat16),
            pltpu.VMEM(row_shape, jnp.bfloat16),
            pltpu.VMEM(col_shape, jnp.bfloat16),
            pltpu.VMEM(col_shape, jnp.bfloat16),
        ],
        compiler_params=pltpu.CompilerParams(vmem_limit_bytes=48 * 1024 * 1024),
        cost_estimate=pl.CostEstimate(
            flops=12 * kernels * step * rows * cols * 512,
            bytes_accessed=4 * step * cols * (padded_rows + kernels * rows),
            transcendentals=0,
        ),
    )(up, middle, down, left, right, row_band, col_band, free_lanes, *so_far)


def legendre(coords):
    return jnp.stack(
        [
            jnp.ones_like(coords),
            coords,
            1.5 * coords * coords - 0.5,
            2.5 * coords * coords * coords - 1.5 * coords,
        ]
    )


def channel_coords(indices, channel_total):
    return 2.0 * indices.astype(jnp.float32) / (channel_total - 1) - 1.0


def invert_small(matrices):
    dimension = matrices.shape[-1]
    identity = jnp.broadcast_to(jnp.eye(dimension, dtype=matrices.dtype), matrices.shape)
    augmented = jnp.concatenate([matrices, identity], axis=2)
    for pivot_at in range(dimension):
        pivot_row = augmented[:, pivot_at, :] / augmented[:, pivot_at, pivot_at : pivot_at + 1]
        updated = augmented - augmented[:, :, pivot_at : pivot_at + 1] * pivot_row[:, None, :]
        chosen = (jnp.arange(dimension) == pivot_at)[None, :, None]
        augmented = jnp.where(chosen, pivot_row[:, None, :], updated)
    return augmented[:, :, dimension:]


def gaussian_taps(kernel_widths):
    offsets = jnp.arange(-HALF, HALF + 1).astype(jnp.float32)
    sigmas = kernel_widths.astype(jnp.float32)
    unscaled = jnp.exp(
        -offsets[None, :] * offsets[None, :] / (2.0 * sigmas[:, None] * sigmas[:, None])
    )
    return unscaled / jnp.sum(unscaled, axis=1, keepdims=True)


def median_three(edge_levels):
    below_level = edge_levels[:, :-2]
    middle = edge_levels[:, 1:-1]
    above_level = edge_levels[:, 2:]
    highest_one = jnp.maximum(jnp.maximum(below_level, middle), above_level)
    lowest_one = jnp.minimum(jnp.minimum(below_level, middle), above_level)
    return below_level + middle + above_level - highest_one - lowest_one


def band_matrices(taps, differences):
    band = jnp.zeros((taps.shape[0],) + differences.shape, jnp.float32)
    for offset in range(2 * HALF + 1):
        band = band + jnp.where(differences == offset, taps[:, offset][:, None, None], 0.0)
    return band


def body(spectral_cube, line_free, bad_flags, kernel_widths):
    tile_count = lax.axis_size("tile")
    tile_at = lax.axis_index("tile")
    chan_at = lax.axis_index("chan")
    sub_count = spectral_cube.shape[1]
    group_size = sub_count * tile_count
    full_rows = spectral_cube.shape[2]
    local_rows = full_rows // tile_count
    local_cols = spectral_cube.shape[3]
    channel_total = line_free.shape[1]
    good_mask = (1 - bad_flags).astype(jnp.float32)
    free_mask = line_free.astype(jnp.float32)
    weights = free_mask * good_mask[None, :]
    basis_all = legendre(channel_coords(jnp.arange(channel_total), channel_total))
    normal_matrix = jnp.einsum("rc,ic,jc->rij", weights, basis_all, basis_all, precision=highest)
    inverse_rows = jnp.repeat(invert_small(normal_matrix), REG, axis=0)
    group_first = chan_at * group_size
    row_first = tile_at * local_rows
    basis_group = lax.dynamic_slice_in_dim(basis_all, group_first, group_size, 1)
    weight_all_rows = jnp.repeat(weights, REG, axis=0)
    inverse_local = lax.dynamic_slice_in_dim(inverse_rows, row_first, local_rows, 0)
    received = lax.all_to_all(spectral_cube, "tile", split_axis=2, concat_axis=1, tiled=True)[0]
    weight_local = lax.dynamic_slice_in_dim(
        lax.dynamic_slice_in_dim(weight_all_rows, row_first, local_rows, 0),
        group_first,
        group_size,
        1,
    )
    slab = 128
    width = 256 if local_cols % 256 == 0 else 128
    sub = 8
    kernel_taps = gaussian_taps(kernel_widths)
    kernels = kernel_taps.shape[0]
    padded_rows = local_rows + 2 * HALF
    column_diff = (
        jnp.arange(width + 2 * slab)[:, None] - jnp.arange(width)[None, :] - slab + HALF
    )
    row_diff = jnp.arange(padded_rows)[None, :] - jnp.arange(local_rows)[:, None]
    col_band = band_matrices(kernel_taps, column_diff)
    row_band = band_matrices(kernel_taps, row_diff)
    same = jnp.eye(sub, dtype=jnp.float32)
    row_band = (
        row_band[:, None, :, :, None] * same[None, :, None, None, :]
    ).reshape(kernels * sub * local_rows, padded_rows * sub)
    free_rows = jnp.repeat(free_mask, REG, axis=0)
    free_local = lax.dynamic_slice_in_dim(
        lax.dynamic_slice_in_dim(free_rows, row_first, local_rows, 0), group_first, group_size, 1
    ).T
    free_lanes = jnp.broadcast_to(free_local[:, :, None], free_local.shape + (128,))
    received, row_band, col_band, free_lanes = lax.optimization_barrier(
        (received, row_band, col_band, free_lanes)
    )
    block_moments = jnp.einsum(
        "ic,chw->ihw", basis_group, received * weight_local.T[:, :, None], precision=highest
    )
    row_share = sum_over(block_moments, "chan")
    coeffs = jnp.einsum("hij,jhw->ihw", inverse_local, row_share, precision=highest)
    continuum = jnp.einsum("ic,ihw->hcw", basis_group, coeffs, precision=highest)
    residual = jnp.transpose(received, (1, 0, 2)) - continuum
    col_size = lax.axis_size("col")
    onward = [(i, i + 1) for i in range(col_size - 1)]
    back = [(j, i) for i, j in onward]
    step = 32 if group_size % 32 == 0 else sub
    smoothed, powers = (), []
    for chunk in range(group_size // step):
        part = residual[:, chunk * step : (chunk + 1) * step, :]
        up, down = neighbour_slabs(part, "tile", 0, HALF)
        if powers:
            up, down, part, powers[-1] = lax.optimization_barrier((up, down, part, powers[-1]))
        last, leading = [
            jnp.concatenate([rows[:, :, edge] for rows in (up, part, down)], axis=0)
            for edge in (slice(local_cols - slab, local_cols), slice(0, slab))
        ]
        left = lax.ppermute(last, "col", onward)
        right = lax.ppermute(leading, "col", back)
        *smoothed, power = smooth_call(
            chunk, up, residual, down, left, right, row_band, col_band, free_lanes, smoothed
        )
        powers.append(jnp.sum(power, axis=2))
    (smoothed,) = smoothed
    power = jnp.concatenate(powers, axis=1)
    below, above = neighbour_slabs(power, "chan", 1, 1)
    edge_powers = jnp.concatenate([below, power, above], axis=1)
    edge_powers = sum_over(sum_over(edge_powers, "col"), "tile", 4)
    counts_all = REG * local_cols * lax.axis_size("col") * jnp.sum(free_mask, axis=0)
    positions = group_first - 1 + jnp.arange(group_size + 2)
    inside = (positions >= 0) & (positions < channel_total)
    counts = lax.dynamic_slice_in_dim(jnp.pad(counts_all, 1), group_first, group_size + 2, 0)
    counts = jnp.where(inside, counts, 1.0)
    edge_levels = jnp.where(inside, jnp.sqrt(edge_powers / counts[None, :] + 1e-06), 0.0)
    noise_floor = median_three(edge_levels)
    good_group = lax.dynamic_slice_in_dim(good_mask, group_first, group_size, 0)
    return smoothed * (good_group[None, :] / noise_floor)[:, :, None, None]


def solution(mesh):
    return jax.shard_map(
        body,
        mesh=mesh,
        in_specs=(P("chan", "tile", "win", "col"), P("win", None), P("win"), P()),
        out_specs=P(None, "chan", ("win", "tile"), "col"),
        check_vma=False,
    )
```

```python
import functools

import jax
import jax.numpy as jnp
from jax import lax
from jax.experimental import pallas as pl
from jax.experimental.pallas import tpu as pltpu
from jax.sharding import PartitionSpec as P

HALF = 8
REG = 16


highest = lax.Precision.HIGHEST


def neighbour_slabs(shard, axis, dim, width):
    size, length = (lax.axis_size(axis), shard.shape[dim])
    up = [(i, (i + 1) % size) for i in range(size - 1)]
    down = [(j, i) for i, j in up]
    last = lax.slice_in_dim(shard, length - width, length, axis=dim)
    leading = lax.slice_in_dim(shard, 0, width, axis=dim)
    return lax.ppermute(last, axis, up), lax.ppermute(leading, axis, down)


def sum_over(values, axis, most=2):
    size = lax.axis_size(axis)
    if size > most or size & (size - 1):
        return lax.psum(values, axis)
    stride = 1
    while stride < size:
        pairs = [(i, i ^ stride) for i in range(size)]
        values = values + lax.ppermute(values, axis, pairs)
        stride *= 2
    return values


def split(values):
    high = values.astype(jnp.bfloat16)
    return high, (values - high.astype(jnp.float32)).astype(jnp.bfloat16)


def dot3(a, b):
    dot = functools.partial(jnp.dot, preferred_element_type=jnp.float32)
    return dot(a[0], b[0]) + (dot(a[0], b[1]) + dot(a[1], b[0]))


def smooth_kernel(
    sub, up_ref, mid_ref, down_ref, left_ref, right_ref, row_ref, col_ref, free_ref, *rest
):
    out_ref, power_ref, row_high, row_low, col_high, col_low = rest[-6:]
    kernels, channels, rows, cols = out_ref.shape
    slab = left_ref.shape[2]
    width = col_ref.shape[2]

    @pl.when(pl.program_id(0) == 0)
    def _():
        row_high[...], row_low[...] = split(row_ref[...])
        col_high[...], col_low[...] = split(col_ref[...])

    row_pair = (row_high[...], row_low[...])
    smooth_rows = []
    for first in range(0, channels, sub):
        def flat(ref):
            part = ref[:, first : first + sub, :]
            return part.reshape(part.shape[0] * sub, part.shape[2])

        middle = jnp.concatenate([flat(up_ref), flat(mid_ref), flat(down_ref)], axis=0)
        block = jnp.concatenate([flat(left_ref), middle, flat(right_ref)], axis=1)
        smooth_rows.append(split(dot3(row_pair, split(block))))
    size = sub * rows
    for kernel_at in range(kernels):
        part = slice(kernel_at * size, (kernel_at + 1) * size)
        high = jnp.concatenate([pair[0][part] for pair in smooth_rows], axis=0)
        low = jnp.concatenate([pair[1][part] for pair in smooth_rows], axis=0)
        col_pair = (col_high[kernel_at], col_low[kernel_at])
        total = jnp.zeros((channels, rows, 128), jnp.float32)
        for start in range(0, cols, width):
            window = slice(start, start + width + 2 * slab)
            smooth = dot3((high[:, window], low[:, window]), col_pair)
            smooth = smooth.reshape(channels, rows, width)
            out_ref[kernel_at, :, :, start : start + width] = smooth
            for lane in range(0, width, 128):
                piece = smooth[:, :, lane : lane + 128]
                total = total + piece * piece
        power_ref[kernel_at] = jnp.sum(total * free_ref[...], axis=1)


def smooth_call(chunk, up, middle, down, left, right, row_band, col_band, free_lanes, so_far):
    rows, channels, cols = middle.shape
    kernels = col_band.shape[0]
    padded_rows, share, slab = left.shape
    sub = 8
    step = 32 if share % 32 == 0 else sub
    steps = share // step

    def whole(height, width):
        return pl.BlockSpec((height, step, width), lambda i: (0, i, 0))

    row_shape, col_shape = row_band.shape, col_band.shape
    return pl.pallas_call(
        functools.partial(smooth_kernel, sub),
        grid=(steps,),
        out_shape=(
            jax.ShapeDtypeStruct((kernels, channels, rows, cols), jnp.float32),
            jax.ShapeDtypeStruct((kernels, share, 128), jnp.float32),
        ),
        in_specs=[
            whole(HALF, cols),
            pl.BlockSpec((rows, step, cols), lambda i: (0, chunk * steps + i, 0)),
            whole(HALF, cols),
            whole(padded_rows, slab),
            whole(padded_rows, slab),
            pl.BlockSpec(row_shape, lambda i: (0, 0)),
            pl.BlockSpec(col_shape, lambda i: (0, 0, 0)),
            pl.BlockSpec((step, rows, 128), lambda i: (chunk * steps + i, 0, 0)),
        ]
        + [pl.BlockSpec(memory_space=pl.ANY)] * len(so_far),
        out_specs=(
            pl.BlockSpec((kernels, step, rows, cols), lambda i: (0, chunk * steps + i, 0, 0)),
            pl.BlockSpec((kernels, step, 128), lambda i: (0, i, 0)),
        ),
        input_output_aliases={8: 0} if so_far else {},
        scratch_shapes=[
            pltpu.VMEM(row_shape, jnp.bfloat16),
            pltpu.VMEM(row_shape, jnp.bfloat16),
            pltpu.VMEM(col_shape, jnp.bfloat16),
            pltpu.VMEM(col_shape, jnp.bfloat16),
        ],
        compiler_params=pltpu.CompilerParams(vmem_limit_bytes=48 * 1024 * 1024),
        cost_estimate=pl.CostEstimate(
            flops=12 * kernels * share * rows * cols * 512,
            bytes_accessed=4 * share * cols * (padded_rows + kernels * rows),
            transcendentals=0,
        ),
    )(up, middle, down, left, right, row_band, col_band, free_lanes, *so_far)


def legendre(coords):
    return jnp.stack(
        [
            jnp.ones_like(coords),
            coords,
            1.5 * coords * coords - 0.5,
            2.5 * coords * coords * coords - 1.5 * coords,
        ]
    )


def channel_coords(indices, channel_total):
    return 2.0 * indices.astype(jnp.float32) / (channel_total - 1) - 1.0


def invert_small(matrices):
    dimension = matrices.shape[-1]
    identity = jnp.broadcast_to(jnp.eye(dimension, dtype=matrices.dtype), matrices.shape)
    augmented = jnp.concatenate([matrices, identity], axis=2)
    for pivot_at in range(dimension):
        pivot_row = augmented[:, pivot_at, :] / augmented[:, pivot_at, pivot_at : pivot_at + 1]
        updated = augmented - augmented[:, :, pivot_at : pivot_at + 1] * pivot_row[:, None, :]
        chosen = (jnp.arange(dimension) == pivot_at)[None, :, None]
        augmented = jnp.where(chosen, pivot_row[:, None, :], updated)
    return augmented[:, :, dimension:]


def gaussian_taps(kernel_widths):
    offsets = jnp.arange(-HALF, HALF + 1).astype(jnp.float32)
    sigmas = kernel_widths.astype(jnp.float32)
    unscaled = jnp.exp(
        -offsets[None, :] * offsets[None, :] / (2.0 * sigmas[:, None] * sigmas[:, None])
    )
    return unscaled / jnp.sum(unscaled, axis=1, keepdims=True)


def median_three(edge_levels):
    below_level = edge_levels[:, :-2]
    middle = edge_levels[:, 1:-1]
    above_level = edge_levels[:, 2:]
    highest_one = jnp.maximum(jnp.maximum(below_level, middle), above_level)
    lowest_one = jnp.minimum(jnp.minimum(below_level, middle), above_level)
    return below_level + middle + above_level - highest_one - lowest_one


def band_matrices(taps, differences):
    band = jnp.zeros((taps.shape[0],) + differences.shape, jnp.float32)
    for offset in range(2 * HALF + 1):
        band = band + jnp.where(differences == offset, taps[:, offset][:, None, None], 0.0)
    return band


def body(spectral_cube, line_free, bad_flags, kernel_widths):
    tile_count = lax.axis_size("tile")
    tile_at = lax.axis_index("tile")
    chan_at = lax.axis_index("chan")
    sub_count = spectral_cube.shape[1]
    group_size = sub_count * tile_count
    full_rows = spectral_cube.shape[2]
    local_rows = full_rows // tile_count
    local_cols = spectral_cube.shape[3]
    channel_total = line_free.shape[1]
    good_mask = (1 - bad_flags).astype(jnp.float32)
    free_mask = line_free.astype(jnp.float32)
    weights = free_mask * good_mask[None, :]
    basis_all = legendre(channel_coords(jnp.arange(channel_total), channel_total))
    normal_matrix = jnp.einsum("rc,ic,jc->rij", weights, basis_all, basis_all, precision=highest)
    inverse_rows = jnp.repeat(invert_small(normal_matrix), REG, axis=0)
    group_first = chan_at * group_size
    row_first = tile_at * local_rows
    basis_group = lax.dynamic_slice_in_dim(basis_all, group_first, group_size, 1)
    weight_all_rows = jnp.repeat(weights, REG, axis=0)
    inverse_local = lax.dynamic_slice_in_dim(inverse_rows, row_first, local_rows, 0)
    received = lax.all_to_all(spectral_cube, "tile", split_axis=2, concat_axis=1, tiled=True)[0]
    weight_local = lax.dynamic_slice_in_dim(
        lax.dynamic_slice_in_dim(weight_all_rows, row_first, local_rows, 0),
        group_first,
        group_size,
        1,
    )
    slab = 128
    width = 256 if local_cols % 256 == 0 else 128
    sub = 8
    kernel_taps = gaussian_taps(kernel_widths)
    kernels = kernel_taps.shape[0]
    padded_rows = local_rows + 2 * HALF
    column_diff = (
        jnp.arange(width + 2 * slab)[:, None] - jnp.arange(width)[None, :] - slab + HALF
    )
    row_diff = jnp.arange(padded_rows)[None, :] - jnp.arange(local_rows)[:, None]
    col_band = band_matrices(kernel_taps, column_diff)
    row_band = band_matrices(kernel_taps, row_diff)
    same = jnp.eye(sub, dtype=jnp.float32)
    row_band = (
        row_band[:, None, :, :, None] * same[None, :, None, None, :]
    ).reshape(kernels * sub * local_rows, padded_rows * sub)
    free_rows = jnp.repeat(free_mask, REG, axis=0)
    free_local = lax.dynamic_slice_in_dim(
        lax.dynamic_slice_in_dim(free_rows, row_first, local_rows, 0), group_first, group_size, 1
    ).T
    free_lanes = jnp.broadcast_to(free_local[:, :, None], free_local.shape + (128,))
    received, row_band, col_band, free_lanes = lax.optimization_barrier(
        (received, row_band, col_band, free_lanes)
    )
    block_moments = jnp.einsum(
        "ic,chw->ihw", basis_group, received * weight_local.T[:, :, None], precision=highest
    )
    row_share = sum_over(block_moments, "chan")
    coeffs = jnp.einsum("hij,jhw->ihw", inverse_local, row_share, precision=highest)
    continuum = jnp.einsum("ic,ihw->hcw", basis_group, coeffs, precision=highest)
    residual = jnp.transpose(received, (1, 0, 2)) - continuum
    col_size = lax.axis_size("col")
    onward = [(i, i + 1) for i in range(col_size - 1)]
    back = [(j, i) for i, j in onward]
    step = group_size // 2 if group_size % 64 == 0 else group_size
    smoothed, powers = (), []
    for chunk in range(group_size // step):
        part = residual[:, chunk * step : (chunk + 1) * step, :]
        up, down = neighbour_slabs(part, "tile", 0, HALF)
        if powers:
            up, down, part, powers[-1] = lax.optimization_barrier((up, down, part, powers[-1]))
        last, leading = [
            jnp.concatenate([rows[:, :, edge] for rows in (up, part, down)], axis=0)
            for edge in (slice(local_cols - slab, local_cols), slice(0, slab))
        ]
        left = lax.ppermute(last, "col", onward)
        right = lax.ppermute(leading, "col", back)
        *smoothed, power = smooth_call(
            chunk, up, residual, down, left, right, row_band, col_band, free_lanes, smoothed
        )
        powers.append(jnp.sum(power, axis=2))
    (smoothed,) = smoothed
    power = jnp.concatenate(powers, axis=1)
    below, above = neighbour_slabs(power, "chan", 1, 1)
    edge_powers = jnp.concatenate([below, power, above], axis=1)
    edge_powers = sum_over(sum_over(edge_powers, "col"), "tile", 4)
    counts_all = REG * local_cols * lax.axis_size("col") * jnp.sum(free_mask, axis=0)
    positions = group_first - 1 + jnp.arange(group_size + 2)
    inside = (positions >= 0) & (positions < channel_total)
    counts = lax.dynamic_slice_in_dim(jnp.pad(counts_all, 1), group_first, group_size + 2, 0)
    counts = jnp.where(inside, counts, 1.0)
    edge_levels = jnp.where(inside, jnp.sqrt(edge_powers / counts[None, :] + 1e-06), 0.0)
    noise_floor = median_three(edge_levels)
    good_group = lax.dynamic_slice_in_dim(good_mask, group_first, group_size, 0)
    return smoothed * (good_group[None, :] / noise_floor)[:, :, None, None]


def solution(mesh):
    return jax.shard_map(
        body,
        mesh=mesh,
        in_specs=(P("chan", "tile", "win", "col"), P("win", None), P("win"), P()),
        out_specs=P(None, "chan", ("win", "tile"), "col"),
        check_vma=False,
    )
```

```python
import functools

import jax
import jax.numpy as jnp
from jax import lax
from jax.experimental import pallas as pl
from jax.experimental.pallas import tpu as pltpu
from jax.sharding import PartitionSpec as P

HALF = 8
REG = 16


highest = lax.Precision.HIGHEST


def neighbour_slabs(shard, axis, dim, width):
    size, length = (lax.axis_size(axis), shard.shape[dim])
    up = [(i, (i + 1) % size) for i in range(size - 1)]
    down = [(j, i) for i, j in up]
    last = lax.slice_in_dim(shard, length - width, length, axis=dim)
    leading = lax.slice_in_dim(shard, 0, width, axis=dim)
    return lax.ppermute(last, axis, up), lax.ppermute(leading, axis, down)


def sum_over(values, axis, most=2):
    size = lax.axis_size(axis)
    if size > most or size & (size - 1):
        return lax.psum(values, axis)
    stride = 1
    while stride < size:
        pairs = [(i, i ^ stride) for i in range(size)]
        values = values + lax.ppermute(values, axis, pairs)
        stride *= 2
    return values


def split(values):
    high = values.astype(jnp.bfloat16)
    return high, (values - high.astype(jnp.float32)).astype(jnp.bfloat16)


def dot3(a, b):
    dot = functools.partial(jnp.dot, preferred_element_type=jnp.float32)
    return dot(a[0], b[0]) + (dot(a[0], b[1]) + dot(a[1], b[0]))


def smooth_kernel(
    sub, up_ref, mid_ref, down_ref, left_ref, right_ref, row_ref, col_ref, free_ref, *rest
):
    out_ref, power_ref, row_high, row_low, col_high, col_low = rest[-6:]
    kernels, channels, rows, cols = out_ref.shape
    slab = left_ref.shape[2]
    width = col_ref.shape[2]

    @pl.when(pl.program_id(0) == 0)
    def _():
        row_high[...], row_low[...] = split(row_ref[...])
        col_high[...], col_low[...] = split(col_ref[...])

    row_pair = (row_high[...], row_low[...])
    smooth_rows = []
    for first in range(0, channels, sub):
        def flat(ref):
            part = ref[:, first : first + sub, :]
            return part.reshape(part.shape[0] * sub, part.shape[2])

        middle = jnp.concatenate([flat(up_ref), flat(mid_ref), flat(down_ref)], axis=0)
        block = jnp.concatenate([flat(left_ref), middle, flat(right_ref)], axis=1)
        smooth_rows.append(split(dot3(row_pair, split(block))))
    size = sub * rows
    for kernel_at in range(kernels):
        part = slice(kernel_at * size, (kernel_at + 1) * size)
        high = jnp.concatenate([pair[0][part] for pair in smooth_rows], axis=0)
        low = jnp.concatenate([pair[1][part] for pair in smooth_rows], axis=0)
        col_pair = (col_high[kernel_at], col_low[kernel_at])
        total = jnp.zeros((channels, rows, 128), jnp.float32)
        for start in range(0, cols, width):
            window = slice(start, start + width + 2 * slab)
            smooth = dot3((high[:, window], low[:, window]), col_pair)
            smooth = smooth.reshape(channels, rows, width)
            out_ref[kernel_at, :, :, start : start + width] = smooth
            for lane in range(0, width, 128):
                piece = smooth[:, :, lane : lane + 128]
                total = total + piece * piece
        power_ref[kernel_at] = jnp.sum(total * free_ref[...], axis=1)


def smooth_call(chunk, up, middle, down, left, right, row_band, col_band, free_lanes, so_far):
    rows, channels, cols = middle.shape
    kernels = col_band.shape[0]
    padded_rows, share, slab = left.shape
    sub = 8
    step = 32 if share % 32 == 0 else sub
    steps = share // step

    def whole(height, width):
        return pl.BlockSpec((height, step, width), lambda i: (0, i, 0))

    row_shape, col_shape = row_band.shape, col_band.shape
    return pl.pallas_call(
        functools.partial(smooth_kernel, sub),
        grid=(steps,),
        out_shape=(
            jax.ShapeDtypeStruct((kernels, channels, rows, cols), jnp.float32),
            jax.ShapeDtypeStruct((kernels, share, 128), jnp.float32),
        ),
        in_specs=[
            whole(HALF, cols),
            pl.BlockSpec((rows, step, cols), lambda i: (0, chunk * steps + i, 0)),
            whole(HALF, cols),
            whole(padded_rows, slab),
            whole(padded_rows, slab),
            pl.BlockSpec(row_shape, lambda i: (0, 0)),
            pl.BlockSpec(col_shape, lambda i: (0, 0, 0)),
            pl.BlockSpec((step, rows, 128), lambda i: (chunk * steps + i, 0, 0)),
        ]
        + [pl.BlockSpec(memory_space=pl.ANY)] * len(so_far),
        out_specs=(
            pl.BlockSpec((kernels, step, rows, cols), lambda i: (0, chunk * steps + i, 0, 0)),
            pl.BlockSpec((kernels, step, 128), lambda i: (0, i, 0)),
        ),
        input_output_aliases={8: 0} if so_far else {},
        scratch_shapes=[
            pltpu.VMEM(row_shape, jnp.bfloat16),
            pltpu.VMEM(row_shape, jnp.bfloat16),
            pltpu.VMEM(col_shape, jnp.bfloat16),
            pltpu.VMEM(col_shape, jnp.bfloat16),
        ],
        compiler_params=pltpu.CompilerParams(vmem_limit_bytes=48 * 1024 * 1024),
        cost_estimate=pl.CostEstimate(
            flops=12 * kernels * share * rows * cols * 512,
            bytes_accessed=4 * share * cols * (padded_rows + kernels * rows),
            transcendentals=0,
        ),
    )(up, middle, down, left, right, row_band, col_band, free_lanes, *so_far)


def legendre(coords):
    return jnp.stack(
        [
            jnp.ones_like(coords),
            coords,
            1.5 * coords * coords - 0.5,
            2.5 * coords * coords * coords - 1.5 * coords,
        ]
    )


def channel_coords(indices, channel_total):
    return 2.0 * indices.astype(jnp.float32) / (channel_total - 1) - 1.0


def invert_small(matrices):
    dimension = matrices.shape[-1]
    identity = jnp.broadcast_to(jnp.eye(dimension, dtype=matrices.dtype), matrices.shape)
    augmented = jnp.concatenate([matrices, identity], axis=2)
    for pivot_at in range(dimension):
        pivot_row = augmented[:, pivot_at, :] / augmented[:, pivot_at, pivot_at : pivot_at + 1]
        updated = augmented - augmented[:, :, pivot_at : pivot_at + 1] * pivot_row[:, None, :]
        chosen = (jnp.arange(dimension) == pivot_at)[None, :, None]
        augmented = jnp.where(chosen, pivot_row[:, None, :], updated)
    return augmented[:, :, dimension:]


def gaussian_taps(kernel_widths):
    offsets = jnp.arange(-HALF, HALF + 1).astype(jnp.float32)
    sigmas = kernel_widths.astype(jnp.float32)
    unscaled = jnp.exp(
        -offsets[None, :] * offsets[None, :] / (2.0 * sigmas[:, None] * sigmas[:, None])
    )
    return unscaled / jnp.sum(unscaled, axis=1, keepdims=True)


def median_three(edge_levels):
    below_level = edge_levels[:, :-2]
    middle = edge_levels[:, 1:-1]
    above_level = edge_levels[:, 2:]
    highest_one = jnp.maximum(jnp.maximum(below_level, middle), above_level)
    lowest_one = jnp.minimum(jnp.minimum(below_level, middle), above_level)
    return below_level + middle + above_level - highest_one - lowest_one


def band_matrices(taps, differences):
    band = jnp.zeros((taps.shape[0],) + differences.shape, jnp.float32)
    for offset in range(2 * HALF + 1):
        band = band + jnp.where(differences == offset, taps[:, offset][:, None, None], 0.0)
    return band


def body(spectral_cube, line_free, bad_flags, kernel_widths):
    tile_count = lax.axis_size("tile")
    tile_at = lax.axis_index("tile")
    chan_at = lax.axis_index("chan")
    sub_count = spectral_cube.shape[1]
    group_size = sub_count * tile_count
    full_rows = spectral_cube.shape[2]
    local_rows = full_rows // tile_count
    local_cols = spectral_cube.shape[3]
    channel_total = line_free.shape[1]
    good_mask = (1 - bad_flags).astype(jnp.float32)
    free_mask = line_free.astype(jnp.float32)
    weights = free_mask * good_mask[None, :]
    basis_all = legendre(channel_coords(jnp.arange(channel_total), channel_total))
    normal_matrix = jnp.einsum("rc,ic,jc->rij", weights, basis_all, basis_all, precision=highest)
    inverse_rows = jnp.repeat(invert_small(normal_matrix), REG, axis=0)
    group_first = chan_at * group_size
    row_first = tile_at * local_rows
    basis_group = lax.dynamic_slice_in_dim(basis_all, group_first, group_size, 1)
    weight_all_rows = jnp.repeat(weights, REG, axis=0)
    inverse_local = lax.dynamic_slice_in_dim(inverse_rows, row_first, local_rows, 0)
    received = lax.all_to_all(spectral_cube, "tile", split_axis=2, concat_axis=1, tiled=True)[0]
    weight_local = lax.dynamic_slice_in_dim(
        lax.dynamic_slice_in_dim(weight_all_rows, row_first, local_rows, 0),
        group_first,
        group_size,
        1,
    )
    slab = 128
    width = 256 if local_cols % 256 == 0 else 128
    sub = 8
    kernel_taps = gaussian_taps(kernel_widths)
    kernels = kernel_taps.shape[0]
    padded_rows = local_rows + 2 * HALF
    column_diff = (
        jnp.arange(width + 2 * slab)[:, None] - jnp.arange(width)[None, :] - slab + HALF
    )
    row_diff = jnp.arange(padded_rows)[None, :] - jnp.arange(local_rows)[:, None]
    col_band = band_matrices(kernel_taps, column_diff)
    row_band = band_matrices(kernel_taps, row_diff)
    same = jnp.eye(sub, dtype=jnp.float32)
    row_band = (
        row_band[:, None, :, :, None] * same[None, :, None, None, :]
    ).reshape(kernels * sub * local_rows, padded_rows * sub)
    free_rows = jnp.repeat(free_mask, REG, axis=0)
    free_local = lax.dynamic_slice_in_dim(
        lax.dynamic_slice_in_dim(free_rows, row_first, local_rows, 0), group_first, group_size, 1
    ).T
    free_lanes = jnp.broadcast_to(free_local[:, :, None], free_local.shape + (128,))
    received, row_band, col_band, free_lanes = lax.optimization_barrier(
        (received, row_band, col_band, free_lanes)
    )
    block_moments = jnp.einsum(
        "ic,chw->ihw", basis_group, received * weight_local.T[:, :, None], precision=highest
    )
    row_share = sum_over(block_moments, "chan")
    coeffs = jnp.einsum("hij,jhw->ihw", inverse_local, row_share, precision=highest)
    continuum = jnp.einsum("ic,ihw->hcw", basis_group, coeffs, precision=highest)
    residual = jnp.transpose(received, (1, 0, 2)) - continuum
    col_size = lax.axis_size("col")
    onward = [(i, i + 1) for i in range(col_size - 1)]
    back = [(j, i) for i, j in onward]
    step = group_size
    smoothed, powers = (), []
    for chunk in range(group_size // step):
        part = residual[:, chunk * step : (chunk + 1) * step, :]
        up, down = neighbour_slabs(part, "tile", 0, HALF)
        if powers:
            up, down, part, powers[-1] = lax.optimization_barrier((up, down, part, powers[-1]))
        last, leading = [
            jnp.concatenate([rows[:, :, edge] for rows in (up, part, down)], axis=0)
            for edge in (slice(local_cols - slab, local_cols), slice(0, slab))
        ]
        left = lax.ppermute(last, "col", onward)
        right = lax.ppermute(leading, "col", back)
        *smoothed, power = smooth_call(
            chunk, up, residual, down, left, right, row_band, col_band, free_lanes, smoothed
        )
        powers.append(jnp.sum(power, axis=2))
    (smoothed,) = smoothed
    power = jnp.concatenate(powers, axis=1)
    below, above = neighbour_slabs(power, "chan", 1, 1)
    edge_powers = jnp.concatenate([below, power, above], axis=1)
    edge_powers = sum_over(sum_over(edge_powers, "col"), "tile", 4)
    counts_all = REG * local_cols * lax.axis_size("col") * jnp.sum(free_mask, axis=0)
    positions = group_first - 1 + jnp.arange(group_size + 2)
    inside = (positions >= 0) & (positions < channel_total)
    counts = lax.dynamic_slice_in_dim(jnp.pad(counts_all, 1), group_first, group_size + 2, 0)
    counts = jnp.where(inside, counts, 1.0)
    edge_levels = jnp.where(inside, jnp.sqrt(edge_powers / counts[None, :] + 1e-06), 0.0)
    noise_floor = median_three(edge_levels)
    good_group = lax.dynamic_slice_in_dim(good_mask, group_first, group_size, 0)
    return smoothed * (good_group[None, :] / noise_floor)[:, :, None, None]


def solution(mesh):
    return jax.shard_map(
        body,
        mesh=mesh,
        in_specs=(P("chan", "tile", "win", "col"), P("win", None), P("win"), P()),
        out_specs=P(None, "chan", ("win", "tile"), "col"),
        check_vma=False,
    )
```

```python
import functools

import jax
import jax.numpy as jnp
from jax import lax
from jax.experimental import pallas as pl
from jax.experimental.pallas import tpu as pltpu
from jax.sharding import PartitionSpec as P

HALF = 8
REG = 16


highest = lax.Precision.HIGHEST


def neighbour_slabs(shard, axis, dim, width):
    size, length = (lax.axis_size(axis), shard.shape[dim])
    up = [(i, (i + 1) % size) for i in range(size - 1)]
    down = [(j, i) for i, j in up]
    last = lax.slice_in_dim(shard, length - width, length, axis=dim)
    leading = lax.slice_in_dim(shard, 0, width, axis=dim)
    return lax.ppermute(last, axis, up), lax.ppermute(leading, axis, down)


def sum_over(values, axis, most=2):
    size = lax.axis_size(axis)
    if size > most or size & (size - 1):
        return lax.psum(values, axis)
    stride = 1
    while stride < size:
        pairs = [(i, i ^ stride) for i in range(size)]
        values = values + lax.ppermute(values, axis, pairs)
        stride *= 2
    return values


def split(values):
    high = values.astype(jnp.bfloat16)
    return high, (values - high.astype(jnp.float32)).astype(jnp.bfloat16)


def dot3(a, b):
    dot = functools.partial(jnp.dot, preferred_element_type=jnp.float32)
    return dot(a[0], b[0]) + (dot(a[0], b[1]) + dot(a[1], b[0]))


def smooth_kernel(
    sub, up_ref, mid_ref, down_ref, left_ref, right_ref, row_ref, col_ref, free_ref, *rest
):
    out_ref, power_ref, row_high, row_low, col_high, col_low = rest[-6:]
    kernels, channels, rows, cols = out_ref.shape
    slab = left_ref.shape[2]
    width = col_ref.shape[2]

    @pl.when(pl.program_id(0) == 0)
    def _():
        row_high[...], row_low[...] = split(row_ref[...])
        col_high[...], col_low[...] = split(col_ref[...])

    row_pair = (row_high[...], row_low[...])
    smooth_rows = []
    for first in range(0, channels, sub):
        def flat(ref):
            part = ref[:, first : first + sub, :]
            return part.reshape(part.shape[0] * sub, part.shape[2])

        middle = jnp.concatenate([flat(up_ref), flat(mid_ref), flat(down_ref)], axis=0)
        block = jnp.concatenate([flat(left_ref), middle, flat(right_ref)], axis=1)
        smooth_rows.append(split(dot3(row_pair, split(block))))
    size = sub * rows
    for kernel_at in range(kernels):
        part = slice(kernel_at * size, (kernel_at + 1) * size)
        high = jnp.concatenate([pair[0][part] for pair in smooth_rows], axis=0)
        low = jnp.concatenate([pair[1][part] for pair in smooth_rows], axis=0)
        col_pair = (col_high[kernel_at], col_low[kernel_at])
        total = jnp.zeros((channels, rows, 128), jnp.float32)
        for start in range(0, cols, width):
            window = slice(start, start + width + 2 * slab)
            smooth = dot3((high[:, window], low[:, window]), col_pair)
            smooth = smooth.reshape(channels, rows, width)
            out_ref[kernel_at, :, :, start : start + width] = smooth
            for lane in range(0, width, 128):
                piece = smooth[:, :, lane : lane + 128]
                total = total + piece * piece
        power_ref[kernel_at] = jnp.sum(total * free_ref[...], axis=1)


def smooth_call(chunk, up, middle, down, left, right, row_band, col_band, free_lanes, so_far):
    rows, channels, cols = middle.shape
    kernels = col_band.shape[0]
    padded_rows, share, slab = left.shape
    sub = 8
    step = 32 if share % 32 == 0 else sub
    steps = share // step

    def whole(height, width):
        return pl.BlockSpec((height, step, width), lambda i: (0, i, 0))

    row_shape, col_shape = row_band.shape, col_band.shape
    return pl.pallas_call(
        functools.partial(smooth_kernel, sub),
        grid=(steps,),
        out_shape=(
            jax.ShapeDtypeStruct((kernels, channels, rows, cols), jnp.float32),
            jax.ShapeDtypeStruct((kernels, share, 128), jnp.float32),
        ),
        in_specs=[
            whole(HALF, cols),
            pl.BlockSpec((rows, step, cols), lambda i: (0, chunk * steps + i, 0)),
            whole(HALF, cols),
            whole(padded_rows, slab),
            whole(padded_rows, slab),
            pl.BlockSpec(row_shape, lambda i: (0, 0)),
            pl.BlockSpec(col_shape, lambda i: (0, 0, 0)),
            pl.BlockSpec((step, rows, 128), lambda i: (chunk * steps + i, 0, 0)),
        ]
        + [pl.BlockSpec(memory_space=pl.ANY)] * len(so_far),
        out_specs=(
            pl.BlockSpec((kernels, step, rows, cols), lambda i: (0, chunk * steps + i, 0, 0)),
            pl.BlockSpec((kernels, step, 128), lambda i: (0, i, 0)),
        ),
        input_output_aliases={8: 0} if so_far else {},
        scratch_shapes=[
            pltpu.VMEM(row_shape, jnp.bfloat16),
            pltpu.VMEM(row_shape, jnp.bfloat16),
            pltpu.VMEM(col_shape, jnp.bfloat16),
            pltpu.VMEM(col_shape, jnp.bfloat16),
        ],
        compiler_params=pltpu.CompilerParams(vmem_limit_bytes=48 * 1024 * 1024),
        cost_estimate=pl.CostEstimate(
            flops=12 * kernels * share * rows * cols * 512,
            bytes_accessed=4 * share * cols * (padded_rows + kernels * rows),
            transcendentals=0,
        ),
    )(up, middle, down, left, right, row_band, col_band, free_lanes, *so_far)


def legendre(coords):
    return jnp.stack(
        [
            jnp.ones_like(coords),
            coords,
            1.5 * coords * coords - 0.5,
            2.5 * coords * coords * coords - 1.5 * coords,
        ]
    )


def channel_coords(indices, channel_total):
    return 2.0 * indices.astype(jnp.float32) / (channel_total - 1) - 1.0


def invert_small(matrices):
    dimension = matrices.shape[-1]
    identity = jnp.broadcast_to(jnp.eye(dimension, dtype=matrices.dtype), matrices.shape)
    augmented = jnp.concatenate([matrices, identity], axis=2)
    for pivot_at in range(dimension):
        pivot_row = augmented[:, pivot_at, :] / augmented[:, pivot_at, pivot_at : pivot_at + 1]
        updated = augmented - augmented[:, :, pivot_at : pivot_at + 1] * pivot_row[:, None, :]
        chosen = (jnp.arange(dimension) == pivot_at)[None, :, None]
        augmented = jnp.where(chosen, pivot_row[:, None, :], updated)
    return augmented[:, :, dimension:]


def gaussian_taps(kernel_widths):
    offsets = jnp.arange(-HALF, HALF + 1).astype(jnp.float32)
    sigmas = kernel_widths.astype(jnp.float32)
    unscaled = jnp.exp(
        -offsets[None, :] * offsets[None, :] / (2.0 * sigmas[:, None] * sigmas[:, None])
    )
    return unscaled / jnp.sum(unscaled, axis=1, keepdims=True)


def median_three(edge_levels):
    below_level = edge_levels[:, :-2]
    middle = edge_levels[:, 1:-1]
    above_level = edge_levels[:, 2:]
    highest_one = jnp.maximum(jnp.maximum(below_level, middle), above_level)
    lowest_one = jnp.minimum(jnp.minimum(below_level, middle), above_level)
    return below_level + middle + above_level - highest_one - lowest_one


def band_matrices(taps, differences):
    band = jnp.zeros((taps.shape[0],) + differences.shape, jnp.float32)
    for offset in range(2 * HALF + 1):
        band = band + jnp.where(differences == offset, taps[:, offset][:, None, None], 0.0)
    return band


def body(spectral_cube, line_free, bad_flags, kernel_widths):
    tile_count = lax.axis_size("tile")
    tile_at = lax.axis_index("tile")
    chan_at = lax.axis_index("chan")
    sub_count = spectral_cube.shape[1]
    group_size = sub_count * tile_count
    full_rows = spectral_cube.shape[2]
    local_rows = full_rows // tile_count
    local_cols = spectral_cube.shape[3]
    channel_total = line_free.shape[1]
    good_mask = (1 - bad_flags).astype(jnp.float32)
    free_mask = line_free.astype(jnp.float32)
    weights = free_mask * good_mask[None, :]
    basis_all = legendre(channel_coords(jnp.arange(channel_total), channel_total))
    normal_matrix = jnp.einsum("rc,ic,jc->rij", weights, basis_all, basis_all, precision=highest)
    inverse_rows = jnp.repeat(invert_small(normal_matrix), REG, axis=0)
    group_first = chan_at * group_size
    row_first = tile_at * local_rows
    basis_group = lax.dynamic_slice_in_dim(basis_all, group_first, group_size, 1)
    weight_all_rows = jnp.repeat(weights, REG, axis=0)
    inverse_local = lax.dynamic_slice_in_dim(inverse_rows, row_first, local_rows, 0)
    received = lax.all_to_all(spectral_cube, "tile", split_axis=2, concat_axis=1, tiled=True)[0]
    weight_local = lax.dynamic_slice_in_dim(
        lax.dynamic_slice_in_dim(weight_all_rows, row_first, local_rows, 0),
        group_first,
        group_size,
        1,
    )
    slab = 128
    width = 256 if local_cols % 256 == 0 else 128
    sub = 8
    kernel_taps = gaussian_taps(kernel_widths)
    kernels = kernel_taps.shape[0]
    padded_rows = local_rows + 2 * HALF
    column_diff = (
        jnp.arange(width + 2 * slab)[:, None] - jnp.arange(width)[None, :] - slab + HALF
    )
    row_diff = jnp.arange(padded_rows)[None, :] - jnp.arange(local_rows)[:, None]
    col_band = band_matrices(kernel_taps, column_diff)
    row_band = band_matrices(kernel_taps, row_diff)
    same = jnp.eye(sub, dtype=jnp.float32)
    row_band = (
        row_band[:, None, :, :, None] * same[None, :, None, None, :]
    ).reshape(kernels * sub * local_rows, padded_rows * sub)
    free_rows = jnp.repeat(free_mask, REG, axis=0)
    free_local = lax.dynamic_slice_in_dim(
        lax.dynamic_slice_in_dim(free_rows, row_first, local_rows, 0), group_first, group_size, 1
    ).T
    free_lanes = jnp.broadcast_to(free_local[:, :, None], free_local.shape + (128,))
    received, row_band, col_band, free_lanes = lax.optimization_barrier(
        (received, row_band, col_band, free_lanes)
    )
    block_moments = jnp.einsum(
        "ic,chw->ihw", basis_group, received * weight_local.T[:, :, None], precision=highest
    )
    row_share = sum_over(block_moments, "chan")
    coeffs = jnp.einsum("hij,jhw->ihw", inverse_local, row_share, precision=highest)
    continuum = jnp.einsum("ic,ihw->hcw", basis_group, coeffs, precision=highest)
    residual = jnp.transpose(received, (1, 0, 2)) - continuum
    col_size = lax.axis_size("col")
    onward = [(i, i + 1) for i in range(col_size - 1)]
    back = [(j, i) for i, j in onward]
    step = group_size // 2 if group_size % 64 == 0 else group_size
    smoothed, powers = (), []
    for chunk in range(group_size // step):
        part = residual[:, chunk * step : (chunk + 1) * step, :]
        up, down = neighbour_slabs(part, "tile", 0, HALF)
        if powers:
            up, down, powers[-1] = lax.optimization_barrier((up, down, powers[-1]))
        last, leading = [
            jnp.concatenate([rows[:, :, edge] for rows in (up, part, down)], axis=0)
            for edge in (slice(local_cols - slab, local_cols), slice(0, slab))
        ]
        left = lax.ppermute(last, "col", onward)
        right = lax.ppermute(leading, "col", back)
        *smoothed, power = smooth_call(
            chunk, up, residual, down, left, right, row_band, col_band, free_lanes, smoothed
        )
        powers.append(jnp.sum(power, axis=2))
    (smoothed,) = smoothed
    power = jnp.concatenate(powers, axis=1)
    below, above = neighbour_slabs(power, "chan", 1, 1)
    edge_powers = jnp.concatenate([below, power, above], axis=1)
    edge_powers = sum_over(sum_over(edge_powers, "col"), "tile", 4)
    counts_all = REG * local_cols * lax.axis_size("col") * jnp.sum(free_mask, axis=0)
    positions = group_first - 1 + jnp.arange(group_size + 2)
    inside = (positions >= 0) & (positions < channel_total)
    counts = lax.dynamic_slice_in_dim(jnp.pad(counts_all, 1), group_first, group_size + 2, 0)
    counts = jnp.where(inside, counts, 1.0)
    edge_levels = jnp.where(inside, jnp.sqrt(edge_powers / counts[None, :] + 1e-06), 0.0)
    noise_floor = median_three(edge_levels)
    good_group = lax.dynamic_slice_in_dim(good_mask, group_first, group_size, 0)
    return smoothed * (good_group[None, :] / noise_floor)[:, :, None, None]


def solution(mesh):
    return jax.shard_map(
        body,
        mesh=mesh,
        in_specs=(P("chan", "tile", "win", "col"), P("win", None), P("win"), P()),
        out_specs=P(None, "chan", ("win", "tile"), "col"),
        check_vma=False,
    )
```
